32 devices in a mesh: row: 4 (over y, core), col: 2 (over x), depth: 4 (over z).
Axes of the slice: x: 2, y: 2, z: 4, core: 2. Of those that a mesh axis runs over, the one named last changes fastest.
Arguments:
- density: bfloat16 [2048, 2048], P('row', 'col'), may hold values from -0.125 to 0.125
- pattern: int32 [32, 32], P('row', 'col'), may hold values 0 or 1
Outputs:
- square: bfloat16 [2048, 2048], P(('row', 'depth'), 'col')
The draws below stay inside these ranges and needn't reach their ends.
All inputs are finite; a program needn't handle non-finite values. No bound on the sum of `pattern` on one device may be relied on, other than what follows from the above.
Results may differ from the reference program's by a relative error of at most 0.001.
Values may be sent and summed in bfloat16 or wider, within the bound.
A program may use at most 64 MiB of HBM per device.

```python
import jax
import jax.numpy as jnp

BLK = 64
NB = 32
ORDER = 2048


def plant(drawn, rng, least, largest):
    longest = drawn.shape.index(max(drawn.shape))
    spots = []
    for shift in (0, 1):
        where = [jax.random.randint(jax.random.fold_in(rng, axis), (), 0, length) for axis, length in enumerate(drawn.shape)]
        where[longest] = (where[longest] + shift) % drawn.shape[longest]
        spots.append(tuple(where))
    return drawn.at[spots[0]].set(least).at[spots[1]].set(largest)


def block_levels(own_key, shape, pieces, smallest, top_value):
    gain, own = 1.0, jax.random.fold_in(own_key, 6)
    for axis_at, blocks in pieces:
        steps = jnp.exp(jax.random.uniform(jax.random.fold_in(own, axis_at), (blocks,), jnp.float32, smallest / len(pieces), top_value / len(pieces)))
        gain = gain * jnp.repeat(steps, shape[axis_at] // blocks).reshape([-1 if axis == axis_at else 1 for axis in range(len(shape))])
    return gain


def gaussian(rng, shape, spread, limit, split=(), kind=jnp.bfloat16):
    drawn = spread * jax.random.normal(rng, shape, jnp.float32)
    if split:
        drawn = drawn * block_levels(rng, shape, split, -0.22, 0.18)
    return jnp.clip(drawn, -limit, limit).astype(kind)


def setup_inputs(seed: int = 0) -> dict:
    key_of = jax.random.split(jax.random.key(seed), 3)
    return {
        "density": gaussian(key_of[0], (ORDER, ORDER), ORDER ** -0.5, 0.125, ((0, 4), (1, 2))),
        "pattern": plant((jax.random.randint(key_of[1], (NB, NB), 0, 2) < 1).astype(jnp.int32), jax.random.fold_in(key_of[1], 1), 0, 1),
    }


def reference(density, pattern):
    full = jnp.repeat(jnp.repeat(pattern, BLK, axis=0), BLK, axis=1)
    masked = jnp.where(full > 0, density, jnp.zeros_like(density))
    product = jnp.dot(masked, masked, preferred_element_type=jnp.float32)
    return jnp.where(full > 0, product, jnp.zeros_like(product)).astype(jnp.bfloat16)
```

```python
import functools

import jax
import jax.numpy as jnp
from jax import lax
from jax.experimental import pallas as pl
from jax.experimental.pallas import tpu as pltpu
from jax.sharding import PartitionSpec as P

BLK = 64
UNIT = 128
MESH = pl.DeviceIdType.MESH
SIXTEENTHS = (4, 4, 3, 3, 1, 1)


def kernel(
    n_row, n_col, n_depth,
    density, pattern, out,
    raw, cols, left, mask, acc,
    load_sem, x_send, x_recv, y_send, y_recv, z_send, z_recv, own_send, own_recv,
    s_send, s_recv,
):
    rows, width = density.shape
    strip = rows // n_depth
    cores = 2 if n_row % 2 == 0 else 1
    share = 2 if n_depth % 2 == 0 else 1
    n_y = n_row // cores
    part = rows // share
    sizes = [s * (part // 16) for s in SIXTEENTHS]
    starts = [sum(sizes[:i]) for i in range(len(sizes))]
    chunks = len(sizes)
    row, col, depth = lax.axis_index("row"), lax.axis_index("col"), lax.axis_index("depth")
    y, core = row // cores, row % cores
    half = depth % share
    sibling = y * cores + (cores - 1 - core)
    mate = depth - half + (share - 1 - half)

    def y_at(j):
        return lax.rem(y + j, n_y)

    here = (row, col, depth)
    y_peers = [(y_at(j) * cores + core, col, depth) for j in range(1, n_y)]
    x_peers = [(row, lax.rem(col + j, n_col), depth) for j in range(1, n_col)]
    sib = (sibling, col, depth)
    mate_at = (row, col, mate)
    greeted = y_peers + x_peers + [sib] * (cores > 1) + [mate_at] * (share > 1)

    barrier = pltpu.get_barrier_semaphore()
    for peer in greeted:
        pl.semaphore_signal(barrier, inc=1, device_id=peer, device_id_type=MESH)

    load = pltpu.make_async_copy(density, raw, load_sem)
    load.start()

    block_rows, block_cols = pattern.shape
    low = lax.broadcasted_iota(jnp.int32, (block_cols, width), 0) * BLK
    at = lax.broadcasted_iota(jnp.int32, (block_cols, width), 1)
    spread = jnp.where((at >= low) & (at < low + BLK), 1.0, 0.0).astype(jnp.bfloat16)
    mask[...] = jnp.dot(
        pattern[...].astype(jnp.float32).astype(jnp.bfloat16), spread,
        preferred_element_type=jnp.float32,
    )
    load.wait()
    base = pl.multiple_of(row * rows, rows)
    for i in range(block_rows):
        keep = jnp.broadcast_to(mask[i:i + 1, :], (16, width)).astype(jnp.bfloat16)
        for t in range(BLK // 16):
            lo = i * BLK + t * 16
            cols[pl.ds(base + lo, 16), :] = raw[lo:lo + 16, :] * keep
    units_here = width // UNIT
    mine = cols[pl.ds(pl.multiple_of(base + depth * strip, strip), strip), :]
    for u in range(units_here):
        left[col * units_here + u] = mine[:, u * UNIT:(u + 1) * UNIT]

    pl.semaphore_wait(barrier, len(greeted))

    def copy(src, dst, send, recv, to):
        return pltpu.make_async_remote_copy(
            src_ref=src, dst_ref=dst, send_sem=send, recv_sem=recv,
            device_id=to, device_id_type=MESH,
        )

    def piece(r, h, i):
        begin = pl.multiple_of(r * rows + h * part + starts[i], 16)
        return cols.at[pl.ds(begin, sizes[i]), :]

    sent = []
    for i in range(chunks):
        for j in range(1, n_y):
            c = copy(piece(row, half, i), piece(row, half, i),
                     y_send.at[j - 1, i], y_recv.at[j - 1, i], y_peers[j - 1])
            c.start()
            sent.append(c)
    for j in range(1, n_col):
        ref = left.at[pl.ds(col * units_here, units_here)]
        c = copy(ref, ref, x_send.at[j - 1], x_recv.at[j - 1], x_peers[j - 1])
        c.start()
        sent.append(c)
    if cores > 1:
        ref = cols.at[pl.ds(base, rows), :]
        c = copy(ref, ref, own_send, own_recv, sib)
        c.start()
        sent.append(c)

    def arrived(ref, recv):
        copy(ref, ref, own_send, recv, sib).wait_recv()

    def to_sibling(j, h, w, i, r):
        if cores > 1:
            c = copy(piece(r, h, i), piece(r, h, i),
                     s_send.at[j - 1, w, i], s_recv.at[j - 1, w, i], sib)
            c.start()
            sent.append(c)

    def multiply(starts_at):
        total = None
        for begin in starts_at:
            term = jnp.dot(
                left[begin // UNIT],
                cols[pl.ds(pl.multiple_of(begin, UNIT), UNIT), :],
                preferred_element_type=jnp.float32,
            )
            total = term if total is None else total + term
        return total

    def from_y(j):
        return lax.rem(y + n_y - j, n_y)

    def take_y(j, i):
        r = from_y(j) * cores + core
        arrived(piece(r, half, i), y_recv.at[j - 1, i])
        if share > 1:
            c = copy(piece(r, half, i), piece(r, half, i),
                     z_send.at[j - 1, i], z_recv.at[j - 1, i], mate_at)
            c.start()
            sent.append(c)
        to_sibling(j, half, 0, i, r)

    def take_z(j, i):
        if share > 1:
            r = from_y(j) * cores + core
            arrived(piece(r, 1 - half, i), z_recv.at[j - 1, i])
            to_sibling(j, 1 - half, 1, i, r)

    def take_sibling(j, w, i):
        if cores > 1:
            r = from_y(j) * cores + (cores - 1 - core)
            h = half if w == 0 else 1 - half
            arrived(piece(r, h, i), s_recv.at[j - 1, w, i])

    def finish(first, last):
        lo = starts[first] if first < chunks else part
        hi = starts[last] if last < chunks else part
        for i in range(first, last):
            for j in range(1, n_y):
                for w in range(share):
                    take_sibling(j, w, i)
        for j in range(1, n_y):
            begins = []
            for k in range(cores):
                for h in range(share):
                    begins += [(from_y(j) * cores + k) * rows + h * part + q
                               for q in range(lo, hi, UNIT)]
            acc[...] += multiply(begins)

    cut = next(i for i in range(chunks) if starts[i] == part // 2)
    for i in range(chunks):
        for j in range(1, n_y):
            take_y(j, i)
            if i:
                take_z(j, i - 1)
        if i == cut:
            for j in range(1, n_col):
                c = lax.rem(col + n_col - j, n_col)
                arrived(left.at[pl.ds(c * units_here, units_here)], x_recv.at[j - 1])
            if cores > 1:
                arrived(cols.at[pl.ds(sibling * rows, rows), :], own_recv)
            acc[...] = multiply([(y * cores + k) * rows + q
                                 for k in range(cores) for q in range(0, rows, UNIT)])
        if i == cut + 1:
            finish(0, cut)
    for j in range(1, n_y):
        take_z(j, chunks - 1)
    if cut + 1 >= chunks:
        finish(0, cut)
    finish(cut, chunks)

    for b in range(strip // BLK):
        keep = mask[pl.ds(depth * (strip // BLK) + b, 1), :]
        out[b * BLK:(b + 1) * BLK, :] = (acc[b * BLK:(b + 1) * BLK, :] * keep).astype(out.dtype)
    for c in sent:
        c.wait_send()


def shards(n_row, n_col, n_depth, density, pattern):
    rows, width = density.shape
    strip = rows // n_depth
    n_y = n_row // 2 if n_row % 2 == 0 else n_row
    chunks = len(SIXTEENTHS)
    dma = pltpu.SemaphoreType.DMA
    j = max(n_y - 1, 1)
    return pl.pallas_call(
        functools.partial(kernel, n_row, n_col, n_depth),
        out_shape=jax.ShapeDtypeStruct((strip, width), jnp.bfloat16),
        in_specs=[pl.BlockSpec(memory_space=pl.ANY), pl.BlockSpec(memory_space=pltpu.VMEM)],
        out_specs=pl.BlockSpec(memory_space=pltpu.VMEM),
        scratch_shapes=[
            pltpu.VMEM((rows, width), jnp.bfloat16),
            pltpu.VMEM((n_row * rows, width), jnp.bfloat16),
            pltpu.VMEM((n_col * width // UNIT, strip, UNIT), jnp.bfloat16),
            pltpu.VMEM((pattern.shape[0], width), jnp.float32),
            pltpu.VMEM((strip, width), jnp.float32),
            dma(()),
            dma((max(n_col - 1, 1),)), dma((max(n_col - 1, 1),)),
            dma((j, chunks)), dma((j, chunks)),
            dma((j, chunks)), dma((j, chunks)),
            dma(()), dma(()),
            dma((j, 2, chunks)), dma((j, 2, chunks)),
        ],
        compiler_params=pltpu.CompilerParams(
            collective_id=0, has_side_effects=True, vmem_limit_bytes=32 * 1024 * 1024
        ),
    )(density, pattern)


def solution(mesh):
    sizes = [mesh.shape[name] for name in ("row", "col", "depth")]
    return jax.shard_map(
        functools.partial(shards, *sizes),
        mesh=mesh,
        in_specs=(P("row", "col"), P("row", "col")),
        out_specs=P(("row", "depth"), "col"),
        check_vma=False,
    )
```

```python
import functools

import jax
import jax.numpy as jnp
from jax import lax
from jax.experimental import pallas as pl
from jax.experimental.pallas import tpu as pltpu
from jax.sharding import PartitionSpec as P

BLK = 64
UNIT = 128
MESH = pl.DeviceIdType.MESH
SIXTEENTHS = (4, 4, 4, 4)


def kernel(
    n_row, n_col, n_depth,
    density, pattern, out,
    raw, blocks, cols, left, mask, acc,
    load_sem, blocks_sem, x_send, x_recv, y_send, y_recv, z_send, z_recv, own_send, own_recv,
    s_send, s_recv,
):
    rows, width = density.shape
    strip = rows // n_depth
    cores = 2 if n_row % 2 == 0 else 1
    share = 2 if n_depth % 2 == 0 else 1
    n_y = n_row // cores
    part = rows // share
    sizes = [s * (part // 16) for s in SIXTEENTHS]
    starts = [sum(sizes[:i]) for i in range(len(sizes))]
    chunks = len(sizes)
    row, col, depth = lax.axis_index("row"), lax.axis_index("col"), lax.axis_index("depth")
    y, core = row // cores, row % cores
    half = depth % share
    sibling = y * cores + (cores - 1 - core)
    mate = depth - half + (share - 1 - half)

    def y_at(j):
        return lax.rem(y + j, n_y)

    here = (row, col, depth)
    y_peers = [(y_at(j) * cores + core, col, depth) for j in range(1, n_y)]
    x_peers = [(row, lax.rem(col + j, n_col), depth) for j in range(1, n_col)]
    sib = (sibling, col, depth)
    mate_at = (row, col, mate)
    greeted = y_peers + x_peers + [sib] * (cores > 1) + [mate_at] * (share > 1)

    fetch = pltpu.make_async_copy(pattern, blocks, blocks_sem)
    fetch.start()
    barrier = pltpu.get_barrier_semaphore()
    for peer in greeted:
        pl.semaphore_signal(barrier, inc=1, device_id=peer, device_id_type=MESH)

    load = pltpu.make_async_copy(density, raw, load_sem)
    load.start()

    block_rows, block_cols = pattern.shape
    low = lax.broadcasted_iota(jnp.int32, (block_cols, width), 0) * BLK
    at = lax.broadcasted_iota(jnp.int32, (block_cols, width), 1)
    spread = jnp.where((at >= low) & (at < low + BLK), 1.0, 0.0).astype(jnp.bfloat16)
    fetch.wait()
    mask[...] = jnp.dot(
        blocks[...].astype(jnp.float32).astype(jnp.bfloat16), spread,
        preferred_element_type=jnp.float32,
    )
    load.wait()
    base = pl.multiple_of(row * rows, rows)
    for i in range(block_rows):
        keep = jnp.broadcast_to(mask[i:i + 1, :], (16, width)).astype(jnp.bfloat16)
        for t in range(BLK // 16):
            lo = i * BLK + t * 16
            cols[pl.ds(base + lo, 16), :] = raw[lo:lo + 16, :] * keep
    units_here = width // UNIT
    mine = cols[pl.ds(pl.multiple_of(base + depth * strip, strip), strip), :]
    for u in range(units_here):
        left[col * units_here + u] = mine[:, u * UNIT:(u + 1) * UNIT]

    pl.semaphore_wait(barrier, len(greeted))

    def copy(src, dst, send, recv, to):
        return pltpu.make_async_remote_copy(
            src_ref=src, dst_ref=dst, send_sem=send, recv_sem=recv,
            device_id=to, device_id_type=MESH,
        )

    def piece(r, h, i):
        begin = pl.multiple_of(r * rows + h * part + starts[i], 16)
        return cols.at[pl.ds(begin, sizes[i]), :]

    sent = []
    for i in range(chunks):
        for j in range(1, n_y):
            c = copy(piece(row, half, i), piece(row, half, i),
                     y_send.at[j - 1, i], y_recv.at[j - 1, i], y_peers[j - 1])
            c.start()
            sent.append(c)
    for j in range(1, n_col):
        ref = left.at[pl.ds(col * units_here, units_here)]
        c = copy(ref, ref, x_send.at[j - 1], x_recv.at[j - 1], x_peers[j - 1])
        c.start()
        sent.append(c)
    if cores > 1:
        ref = cols.at[pl.ds(base, rows), :]
        c = copy(ref, ref, own_send, own_recv, sib)
        c.start()
        sent.append(c)

    def arrived(ref, recv):
        copy(ref, ref, own_send, recv, sib).wait_recv()

    def to_sibling(j, h, w, i, r):
        if cores > 1:
            c = copy(piece(r, h, i), piece(r, h, i),
                     s_send.at[j - 1, w, i], s_recv.at[j - 1, w, i], sib)
            c.start()
            sent.append(c)

    def multiply(starts_at):
        total = None
        for begin in starts_at:
            term = jnp.dot(
                left[begin // UNIT],
                cols[pl.ds(pl.multiple_of(begin, UNIT), UNIT), :],
                preferred_element_type=jnp.float32,
            )
            total = term if total is None else total + term
        return total

    def from_y(j):
        return lax.rem(y + n_y - j, n_y)

    def take_y(j, i):
        r = from_y(j) * cores + core
        arrived(piece(r, half, i), y_recv.at[j - 1, i])
        if share > 1:
            c = copy(piece(r, half, i), piece(r, half, i),
                     z_send.at[j - 1, i], z_recv.at[j - 1, i], mate_at)
            c.start()
            sent.append(c)
        to_sibling(j, half, 0, i, r)

    def take_z(j, i):
        if share > 1:
            r = from_y(j) * cores + core
            arrived(piece(r, 1 - half, i), z_recv.at[j - 1, i])
            to_sibling(j, 1 - half, 1, i, r)

    def take_sibling(j, w, i):
        if cores > 1:
            r = from_y(j) * cores + (cores - 1 - core)
            h = half if w == 0 else 1 - half
            arrived(piece(r, h, i), s_recv.at[j - 1, w, i])

    def finish(first, last):
        lo = starts[first] if first < chunks else part
        hi = starts[last] if last < chunks else part
        for i in range(first, last):
            for j in range(1, n_y):
                for w in range(share):
                    take_sibling(j, w, i)
        for j in range(1, n_y):
            begins = []
            for k in range(cores):
                for h in range(share):
                    begins += [(from_y(j) * cores + k) * rows + h * part + q
                               for q in range(lo, hi, UNIT)]
            acc[...] += multiply(begins)

    cut = next(i for i in range(chunks) if starts[i] == part // 2)
    for i in range(chunks):
        for j in range(1, n_y):
            take_y(j, i)
            if i:
                take_z(j, i - 1)
        if i == cut:
            for j in range(1, n_col):
                c = lax.rem(col + n_col - j, n_col)
                arrived(left.at[pl.ds(c * units_here, units_here)], x_recv.at[j - 1])
            if cores > 1:
                arrived(cols.at[pl.ds(sibling * rows, rows), :], own_recv)
            acc[...] = multiply([(y * cores + k) * rows + q
                                 for k in range(cores) for q in range(0, rows, UNIT)])
        if i == cut + 1:
            finish(0, cut)
    for j in range(1, n_y):
        take_z(j, chunks - 1)
    if cut + 1 >= chunks:
        finish(0, cut)
    finish(cut, chunks)

    for b in range(strip // BLK):
        keep = mask[pl.ds(depth * (strip // BLK) + b, 1), :]
        out[b * BLK:(b + 1) * BLK, :] = (acc[b * BLK:(b + 1) * BLK, :] * keep).astype(out.dtype)
    for c in sent:
        c.wait_send()


def shards(n_row, n_col, n_depth, density, pattern):
    rows, width = density.shape
    strip = rows // n_depth
    n_y = n_row // 2 if n_row % 2 == 0 else n_row
    chunks = len(SIXTEENTHS)
    dma = pltpu.SemaphoreType.DMA
    j = max(n_y - 1, 1)
    return pl.pallas_call(
        functools.partial(kernel, n_row, n_col, n_depth),
        out_shape=jax.ShapeDtypeStruct((strip, width), jnp.bfloat16),
        in_specs=[pl.BlockSpec(memory_space=pltpu.HBM), pl.BlockSpec(memory_space=pltpu.HBM)],
        out_specs=pl.BlockSpec(memory_space=pltpu.VMEM),
        scratch_shapes=[
            pltpu.VMEM((rows, width), jnp.bfloat16),
            pltpu.VMEM(pattern.shape, jnp.int32),
            pltpu.VMEM((n_row * rows, width), jnp.bfloat16),
            pltpu.VMEM((n_col * width // UNIT, strip, UNIT), jnp.bfloat16),
            pltpu.VMEM((pattern.shape[0], width), jnp.float32),
            pltpu.VMEM((strip, width), jnp.float32),
            dma(()), dma(()),
            dma((max(n_col - 1, 1),)), dma((max(n_col - 1, 1),)),
            dma((j, chunks)), dma((j, chunks)),
            dma((j, chunks)), dma((j, chunks)),
            dma(()), dma(()),
            dma((j, 2, chunks)), dma((j, 2, chunks)),
        ],
        compiler_params=pltpu.CompilerParams(
            collective_id=0, has_side_effects=True, vmem_limit_bytes=60 * 1024 * 1024
        ),
    )(density, pattern)


def solution(mesh):
    sizes = [mesh.shape[name] for name in ("row", "col", "depth")]
    return jax.shard_map(
        functools.partial(shards, *sizes),
        mesh=mesh,
        in_specs=(P("row", "col"), P("row", "col")),
        out_specs=P(("row", "depth"), "col"),
        check_vma=False,
    )
```

```python
import functools

import jax
import jax.numpy as jnp
from jax import lax
from jax.experimental import pallas as pl
from jax.experimental.pallas import tpu as pltpu
from jax.sharding import PartitionSpec as P

BLK = 64
LANES = 128
STEPS = 2
AHEAD = 2
MESH = pl.DeviceIdType.MESH


def layout(n_row, n_depth):
    cores = 2 if n_row % 2 == 0 else 1
    share = 2 if n_depth % 2 == 0 else 1
    return cores, share, n_row // cores


def kernel(
    n_row, n_col, n_depth,
    density, pattern, out,
    raw_cols, raw_left, blocks, cols, left, mask, mask_tiles, given, made,
    load_sem, x_send, x_recv, y_send, y_recv, z_send, z_recv, own_send, own_recv,
    s_send, s_recv, o_send, o_recv,
):
    rows, width = density.shape
    strip = rows // n_depth
    cores, share, n_y = layout(n_row, n_depth)
    pair = strip * share
    tiles = width // share // LANES
    row, col, depth = lax.axis_index("row"), lax.axis_index("col"), lax.axis_index("depth")
    y, core = row // cores, row % cores
    half = depth % share
    sibling = y * cores + (cores - 1 - core)
    mate = depth - half + (share - 1 - half)

    y_peers = [(lax.rem(y + j, n_y) * cores + core, col, depth) for j in range(1, n_y)]
    x_peers = [(row, lax.rem(col + j, n_col), depth) for j in range(1, n_col)]
    sib = (sibling, col, depth)
    mate_at = (row, col, mate)
    greeted = y_peers + x_peers + [sib] * (cores > 1) + [mate_at] * (share > 1)

    pair_base = pl.multiple_of((depth - half) * strip, pair)
    loads = [pltpu.make_async_copy(pattern, blocks, load_sem.at[0])]
    for t in range(tiles):
        lane = pl.multiple_of((half * tiles + t) * LANES, LANES)
        loads.append(pltpu.make_async_copy(
            density.at[:, pl.ds(lane, LANES)], raw_cols.at[t], load_sem.at[1 + t]))
    loads.append(pltpu.make_async_copy(
        density.at[pl.ds(pair_base, pair), :], raw_left, load_sem.at[1 + tiles]))
    for c in loads:
        c.start()
    barrier = pltpu.get_barrier_semaphore()
    for peer in greeted:
        pl.semaphore_signal(barrier, inc=1, device_id=peer, device_id_type=MESH)

    block_rows, block_cols = pattern.shape
    low = lax.broadcasted_iota(jnp.int32, (block_cols, width), 0) * BLK
    at = lax.broadcasted_iota(jnp.int32, (block_cols, width), 1)
    spread = jnp.where((at >= low) & (at < low + BLK), 1.0, 0.0).astype(jnp.bfloat16)
    loads[0].wait()
    wide = jnp.dot(
        blocks[...].astype(jnp.float32).astype(jnp.bfloat16), spread,
        preferred_element_type=jnp.float32,
    )
    mask[...] = wide
    for t in range(share * tiles):
        mask_tiles[t] = wide[:, t * LANES:(t + 1) * LANES]
    base = pl.multiple_of(row * rows, rows)
    for t in range(tiles):
        loads[1 + t].wait()
        for i in range(block_rows):
            keep = mask_tiles[half * tiles + t, i:i + 1, :]
            keep = jnp.broadcast_to(keep, (BLK, LANES)).astype(jnp.bfloat16)
            cols[t, pl.ds(base + i * BLK, BLK), :] = raw_cols[t, i * BLK:(i + 1) * BLK, :] * keep

    pl.semaphore_wait(barrier, len(greeted))

    def copy(src, dst, send, recv, to):
        return pltpu.make_async_remote_copy(
            src_ref=src, dst_ref=dst, send_sem=send, recv_sem=recv,
            device_id=to, device_id_type=MESH,
        )

    def arrived(ref, recv):
        copy(ref, ref, own_send, recv, sib).wait_recv()

    def piece(r, t):
        return cols.at[t, pl.ds(pl.multiple_of(r * rows, rows), rows), :]

    sent, flying = [], {}

    def send(*args):
        c = copy(*args)
        c.start()
        sent.append(c)

    def start_y(t):
        for j in range(1, n_y):
            c = copy(piece(row, t), piece(row, t), y_send.at[j - 1, t], y_recv.at[j - 1, t],
                     y_peers[j - 1])
            c.start()
            flying[t, j] = c

    for t in range(min(AHEAD, tiles)):
        start_y(t)
    if cores > 1:
        ref = cols.at[:, pl.ds(base, rows), :]
        send(ref, ref, own_send, own_recv, sib)

    loads[1 + tiles].wait()
    first = depth - half
    for b in range(pair // BLK):
        keep = mask[pl.ds(first * (strip // BLK) + b, 1), :]
        keep = jnp.broadcast_to(keep, (16, width)).astype(jnp.bfloat16)
        for q in range(b * BLK, (b + 1) * BLK, 16):
            left[q:q + 16, pl.ds(pl.multiple_of(col * width, width), width)] = (
                raw_left[q:q + 16, :] * keep)

    step = width // STEPS

    def slab(c, h, k):
        return left.at[pl.ds(pl.multiple_of(h * strip, strip), strip),
                       pl.ds(pl.multiple_of(c * width + k * step, step), step)]

    for k in range(STEPS):
        for j in range(1, n_col):
            send(slab(col, half, k), slab(col, half, k), x_send.at[j - 1, k],
                 x_recv.at[j - 1, k], x_peers[j - 1])

    def take_x(j, k):
        c = lax.rem(col + n_col - j, n_col)
        arrived(slab(c, half, k), x_recv.at[j - 1, k])
        if share > 1:
            send(slab(c, half, k), slab(c, half, k), z_send.at[j - 1, k],
                 z_recv.at[j - 1, k], mate_at)

    def take_z(j, k):
        if share > 1:
            c = lax.rem(col + n_col - j, n_col)
            arrived(slab(c, 1 - half, k), z_recv.at[j - 1, k])

    def take_y(j, t):
        r = lax.rem(y + n_y - j, n_y) * cores + core
        arrived(piece(r, t), y_recv.at[j - 1, t])
        if cores > 1:
            send(piece(r, t), piece(r, t), s_send.at[j - 1, t], s_recv.at[j - 1, t], sib)

    def make(t):
        if cores > 1:
            for j in range(1, n_y):
                r = lax.rem(y + n_y - j, n_y) * cores + (cores - 1 - core)
                arrived(piece(r, t), s_recv.at[j - 1, t])
        tile = half * tiles + t
        blocks_here = strip // BLK
        for s in range(share):
            who = (1 - half) if s == 0 and share > 1 else half
            begin = pl.multiple_of(who * strip, strip)
            product = jnp.dot(left[pl.ds(begin, strip), :], cols[t],
                              preferred_element_type=jnp.float32)
            for b in range(blocks_here):
                keep = mask_tiles[tile, pl.ds((first + who) * blocks_here + b, 1), :]
                value = (product[b * BLK:(b + 1) * BLK, :] * keep).astype(out.dtype)
                if s == 0 and share > 1:
                    given[t, b * BLK:(b + 1) * BLK, :] = value
                else:
                    made[tile, b * BLK:(b + 1) * BLK, :] = value
            if s == 0 and share > 1:
                send(given.at[t], made.at[tile], o_send.at[t], o_recv.at[t], mate_at)

    for t in range(tiles):
        for j in range(1, n_y):
            take_y(j, t)
            flying[t, j].wait_send()
        if t + AHEAD < tiles:
            start_y(t + AHEAD)
        if t < STEPS:
            for j in range(1, n_col):
                take_x(j, t)
        if t == tiles - 2:
            for k in range(STEPS):
                for j in range(1, n_col):
                    take_z(j, k)
            if cores > 1:
                arrived(cols.at[:, pl.ds(pl.multiple_of(sibling * rows, rows), rows), :], own_recv)
            for q in range(tiles - 1):
                make(q)
    make(tiles - 1)
    if share > 1:
        for t in range(tiles):
            arrived(made.at[(1 - half) * tiles + t], o_recv.at[t])
    for t in range(share * tiles):
        out[:, t * LANES:(t + 1) * LANES] = made[t]
    for c in sent:
        c.wait_send()


def shards(n_row, n_col, n_depth, density, pattern):
    rows, width = density.shape
    strip = rows // n_depth
    cores, share, n_y = layout(n_row, n_depth)
    tiles = width // share // LANES
    dma = pltpu.SemaphoreType.DMA
    i, j = max(n_col - 1, 1), max(n_y - 1, 1)
    bf16 = jnp.bfloat16
    return pl.pallas_call(
        functools.partial(kernel, n_row, n_col, n_depth),
        out_shape=jax.ShapeDtypeStruct((strip, width), bf16),
        in_specs=[pl.BlockSpec(memory_space=pltpu.HBM)] * 2,
        out_specs=pl.BlockSpec(memory_space=pltpu.VMEM),
        scratch_shapes=[
            pltpu.VMEM((tiles, rows, LANES), bf16),
            pltpu.VMEM((share * strip, width), bf16),
            pltpu.VMEM(pattern.shape, jnp.int32),
            pltpu.VMEM((tiles, n_row * rows, LANES), bf16),
            pltpu.VMEM((share * strip, n_col * width), bf16),
            pltpu.VMEM((pattern.shape[0], width), jnp.float32),
            pltpu.VMEM((share * tiles, pattern.shape[0], LANES), jnp.float32),
            pltpu.VMEM((tiles, strip, LANES), bf16),
            pltpu.VMEM((share * tiles, strip, LANES), bf16),
            dma((tiles + 2,)),
            dma((i, STEPS)), dma((i, STEPS)),
            dma((j, tiles)), dma((j, tiles)),
            dma((i, STEPS)), dma((i, STEPS)),
            dma(()), dma(()),
            dma((j, tiles)), dma((j, tiles)),
            dma((tiles,)), dma((tiles,)),
        ],
        compiler_params=pltpu.CompilerParams(
            collective_id=0, has_side_effects=True, vmem_limit_bytes=60 * 1024 * 1024
        ),
    )(density, pattern)


def solution(mesh):
    sizes = [mesh.shape[name] for name in ("row", "col", "depth")]
    return jax.shard_map(
        functools.partial(shards, *sizes),
        mesh=mesh,
        in_specs=(P("row", "col"), P("row", "col")),
        out_specs=P(("row", "depth"), "col"),
        check_vma=False,
    )
```

```python
import functools

import jax
import jax.numpy as jnp
from jax import lax
from jax.experimental import pallas as pl
from jax.experimental.pallas import tpu as pltpu
from jax.sharding import PartitionSpec as P

BLK = 64
LANES = 128
STEPS = 4
EARLY = 2
AHEAD = 2
MESH = pl.DeviceIdType.MESH


def layout(n_row, n_depth):
    cores = 2 if n_row % 2 == 0 else 1
    share = 2 if n_depth % 2 == 0 else 1
    return cores, share, n_row // cores


def kernel(
    n_row, n_col, n_depth,
    density, pattern, out,
    raw_cols, raw_left, blocks, cols, left, mask, mask_tiles, given, made,
    load_sem, x_send, x_recv, y_send, y_recv, z_send, z_recv, own_send, own_recv,
    s_send, s_recv, o_send, o_recv,
):
    rows, width = density.shape
    strip = rows // n_depth
    cores, share, n_y = layout(n_row, n_depth)
    pair = strip * share
    tiles = width // share // LANES
    row, col, depth = lax.axis_index("row"), lax.axis_index("col"), lax.axis_index("depth")
    y, core = row // cores, row % cores
    half = depth % share
    sibling = y * cores + (cores - 1 - core)
    mate = depth - half + (share - 1 - half)

    y_peers = [(lax.rem(y + j, n_y) * cores + core, col, depth) for j in range(1, n_y)]
    x_peers = [(row, lax.rem(col + j, n_col), depth) for j in range(1, n_col)]
    sib = (sibling, col, depth)
    mate_at = (row, col, mate)
    greeted = y_peers + x_peers + [sib] * (cores > 1) + [mate_at] * (share > 1)

    pair_base = pl.multiple_of((depth - half) * strip, pair)
    loads = [pltpu.make_async_copy(pattern, blocks, load_sem.at[0])]
    for t in range(tiles):
        lane = pl.multiple_of((half * tiles + t) * LANES, LANES)
        loads.append(pltpu.make_async_copy(
            density.at[:, pl.ds(lane, LANES)], raw_cols.at[t], load_sem.at[1 + t]))
    loads.append(pltpu.make_async_copy(
        density.at[pl.ds(pair_base, pair), :], raw_left, load_sem.at[1 + tiles]))
    for c in loads:
        c.start()
    barrier = pltpu.get_barrier_semaphore()
    for peer in greeted:
        pl.semaphore_signal(barrier, inc=1, device_id=peer, device_id_type=MESH)

    block_rows, block_cols = pattern.shape
    low = lax.broadcasted_iota(jnp.int32, (block_cols, width), 0) * BLK
    at = lax.broadcasted_iota(jnp.int32, (block_cols, width), 1)
    spread = jnp.where((at >= low) & (at < low + BLK), 1.0, 0.0).astype(jnp.bfloat16)
    loads[0].wait()
    wide = jnp.dot(
        blocks[...].astype(jnp.float32).astype(jnp.bfloat16), spread,
        preferred_element_type=jnp.float32,
    )
    mask[...] = wide
    for t in range(share * tiles):
        mask_tiles[t] = wide[:, t * LANES:(t + 1) * LANES]
    base = pl.multiple_of(row * rows, rows)
    for t in range(tiles):
        loads[1 + t].wait()
        for i in range(block_rows):
            keep = mask_tiles[half * tiles + t, i:i + 1, :]
            keep = jnp.broadcast_to(keep, (BLK, LANES)).astype(jnp.bfloat16)
            cols[t, pl.ds(base + i * BLK, BLK), :] = raw_cols[t, i * BLK:(i + 1) * BLK, :] * keep

    pl.semaphore_wait(barrier, len(greeted))

    def copy(src, dst, send, recv, to):
        return pltpu.make_async_remote_copy(
            src_ref=src, dst_ref=dst, send_sem=send, recv_sem=recv,
            device_id=to, device_id_type=MESH,
        )

    def arrived(ref, recv):
        copy(ref, ref, own_send, recv, sib).wait_recv()

    def piece(r, t):
        return cols.at[t, pl.ds(pl.multiple_of(r * rows, rows), rows), :]

    sent, flying = [], {}

    def send(*args):
        c = copy(*args)
        c.start()
        sent.append(c)

    def start_y(t):
        for j in range(1, n_y):
            c = copy(piece(row, t), piece(row, t), y_send.at[j - 1, t], y_recv.at[j - 1, t],
                     y_peers[j - 1])
            c.start()
            flying[t, j] = c

    for t in range(min(AHEAD, tiles)):
        start_y(t)
    if cores > 1:
        ref = cols.at[:, pl.ds(base, rows), :]
        send(ref, ref, own_send, own_recv, sib)

    loads[1 + tiles].wait()
    first = depth - half
    for b in range(pair // BLK):
        keep = mask[pl.ds(first * (strip // BLK) + b, 1), :]
        keep = jnp.broadcast_to(keep, (16, width)).astype(jnp.bfloat16)
        for q in range(b * BLK, (b + 1) * BLK, 16):
            left[q:q + 16, pl.ds(pl.multiple_of(col * width, width), width)] = (
                raw_left[q:q + 16, :] * keep)

    step = width // STEPS

    def slab(c, h, k):
        return left.at[pl.ds(pl.multiple_of(h * strip, strip), strip),
                       pl.ds(pl.multiple_of(c * width + k * step, step), step)]

    for k in range(STEPS):
        for j in range(1, n_col):
            send(slab(col, half, k), slab(col, half, k), x_send.at[j - 1, k],
                 x_recv.at[j - 1, k], x_peers[j - 1])

    def take_x(j, k):
        c = lax.rem(col + n_col - j, n_col)
        arrived(slab(c, half, k), x_recv.at[j - 1, k])
        if share > 1:
            send(slab(c, half, k), slab(c, half, k), z_send.at[j - 1, k],
                 z_recv.at[j - 1, k], mate_at)

    def take_z(j, k):
        if share > 1:
            c = lax.rem(col + n_col - j, n_col)
            arrived(slab(c, 1 - half, k), z_recv.at[j - 1, k])

    def take_y(j, t):
        r = lax.rem(y + n_y - j, n_y) * cores + core
        arrived(piece(r, t), y_recv.at[j - 1, t])
        if cores > 1:
            send(piece(r, t), piece(r, t), s_send.at[j - 1, t], s_recv.at[j - 1, t], sib)

    def make(t):
        if cores > 1:
            for j in range(1, n_y):
                r = lax.rem(y + n_y - j, n_y) * cores + (cores - 1 - core)
                arrived(piece(r, t), s_recv.at[j - 1, t])
        tile = half * tiles + t
        blocks_here = strip // BLK
        for s in range(share):
            who = (1 - half) if s == 0 and share > 1 else half
            begin = pl.multiple_of(who * strip, strip)
            product = jnp.dot(left[pl.ds(begin, strip), :], cols[t],
                              preferred_element_type=jnp.float32)
            for b in range(blocks_here):
                keep = mask_tiles[tile, pl.ds((first + who) * blocks_here + b, 1), :]
                value = (product[b * BLK:(b + 1) * BLK, :] * keep).astype(out.dtype)
                if s == 0 and share > 1:
                    given[t, b * BLK:(b + 1) * BLK, :] = value
                else:
                    made[tile, b * BLK:(b + 1) * BLK, :] = value
            if s == 0 and share > 1:
                send(given.at[t], made.at[tile], o_send.at[t], o_recv.at[t], mate_at)

    def forward_x(lo, hi):
        for k in range(lo, min(hi, STEPS)):
            for j in range(1, n_col):
                take_x(j, k)

    def settle():
        for k in range(STEPS):
            for j in range(1, n_col):
                take_z(j, k)
        if cores > 1:
            arrived(cols.at[:, pl.ds(pl.multiple_of(sibling * rows, rows), rows), :], own_recv)

    per = STEPS // 2
    for t in range(tiles):
        if t < 2:
            forward_x(t * per, t * per + per // 2)
        if t == tiles - 1:
            settle()
            for q in range(EARLY):
                make(q)
        for j in range(1, n_y):
            take_y(j, t)
            flying[t, j].wait_send()
        if t + AHEAD < tiles:
            start_y(t + AHEAD)
        if t < 2:
            forward_x(t * per + per // 2, t * per + per)
    for q in range(EARLY, tiles - 1):
        make(q)
    make(tiles - 1)
    if share > 1:
        for t in range(tiles):
            arrived(made.at[(1 - half) * tiles + t], o_recv.at[t])
    for t in range(share * tiles):
        out[:, t * LANES:(t + 1) * LANES] = made[t]
    for c in sent:
        c.wait_send()


def shards(n_row, n_col, n_depth, density, pattern):
    rows, width = density.shape
    strip = rows // n_depth
    cores, share, n_y = layout(n_row, n_depth)
    tiles = width // share // LANES
    dma = pltpu.SemaphoreType.DMA
    i, j = max(n_col - 1, 1), max(n_y - 1, 1)
    bf16 = jnp.bfloat16
    density = pltpu.with_memory_space_constraint(density, pltpu.HBM)
    pattern = pltpu.with_memory_space_constraint(pattern, pltpu.HBM)
    return pl.pallas_call(
        functools.partial(kernel, n_row, n_col, n_depth),
        out_shape=jax.ShapeDtypeStruct((strip, width), bf16),
        in_specs=[pl.BlockSpec(memory_space=pltpu.HBM)] * 2,
        out_specs=pl.BlockSpec(memory_space=pltpu.VMEM),
        scratch_shapes=[
            pltpu.VMEM((tiles, rows, LANES), bf16),
            pltpu.VMEM((share * strip, width), bf16),
            pltpu.VMEM(pattern.shape, jnp.int32),
            pltpu.VMEM((tiles, n_row * rows, LANES), bf16),
            pltpu.VMEM((share * strip, n_col * width), bf16),
            pltpu.VMEM((pattern.shape[0], width), jnp.float32),
            pltpu.VMEM((share * tiles, pattern.shape[0], LANES), jnp.float32),
            pltpu.VMEM((tiles, strip, LANES), bf16),
            pltpu.VMEM((share * tiles, strip, LANES), bf16),
            dma((tiles + 2,)),
            dma((i, STEPS)), dma((i, STEPS)),
            dma((j, tiles)), dma((j, tiles)),
            dma((i, STEPS)), dma((i, STEPS)),
            dma(()), dma(()),
            dma((j, tiles)), dma((j, tiles)),
            dma((tiles,)), dma((tiles,)),
        ],
        compiler_params=pltpu.CompilerParams(
            collective_id=0, has_side_effects=True, vmem_limit_bytes=32 * 1024 * 1024
        ),
    )(density, pattern)


def solution(mesh):
    sizes = [mesh.shape[name] for name in ("row", "col", "depth")]
    return jax.shard_map(
        functools.partial(shards, *sizes),
        mesh=mesh,
        in_specs=(P("row", "col"), P("row", "col")),
        out_specs=P(("row", "depth"), "col"),
        check_vma=False,
    )
```

```python
import functools

import jax
import jax.numpy as jnp
from jax import lax
from jax.experimental import pallas as pl
from jax.experimental.pallas import tpu as pltpu
from jax.sharding import PartitionSpec as P

BLK = 64
LANES = 128
STEPS = 4
EARLY = 2
AHEAD = 2
MESH = pl.DeviceIdType.MESH


def layout(n_row, n_depth):
    cores = 2 if n_row % 2 == 0 else 1
    share = 2 if n_depth % 2 == 0 else 1
    return cores, share, n_row // cores


def kernel(
    n_row, n_col, n_depth,
    density, pattern, out,
    raw_cols, raw_left, blocks, cols, left, mask, mask_tiles, given, made,
    load_sem, x_send, x_recv, y_send, y_recv, z_send, z_recv, own_send, own_recv,
    s_send, s_recv, o_send, o_recv,
):
    rows, width = density.shape
    strip = rows // n_depth
    cores, share, n_y = layout(n_row, n_depth)
    pair = strip * share
    tiles = width // share // LANES
    row, col, depth = lax.axis_index("row"), lax.axis_index("col"), lax.axis_index("depth")
    y, core = row // cores, row % cores
    half = depth % share
    sibling = y * cores + (cores - 1 - core)
    mate = depth - half + (share - 1 - half)

    y_peers = [(lax.rem(y + j, n_y) * cores + core, col, depth) for j in range(1, n_y)]
    x_peers = [(row, lax.rem(col + j, n_col), depth) for j in range(1, n_col)]
    sib = (sibling, col, depth)
    mate_at = (row, col, mate)
    greeted = y_peers + x_peers + [sib] * (cores > 1) + [mate_at] * (share > 1)

    pair_base = pl.multiple_of((depth - half) * strip, pair)
    loads = [pltpu.make_async_copy(pattern, blocks, load_sem.at[0])]
    for t in range(tiles):
        lane = pl.multiple_of((half * tiles + t) * LANES, LANES)
        loads.append(pltpu.make_async_copy(
            density.at[:, pl.ds(lane, LANES)], raw_cols.at[t], load_sem.at[1 + t]))
    loads.append(pltpu.make_async_copy(
        density.at[pl.ds(pair_base, pair), :], raw_left, load_sem.at[1 + tiles]))
    for c in loads:
        c.start()
    barrier = pltpu.get_barrier_semaphore()
    for peer in greeted:
        pl.semaphore_signal(barrier, inc=1, device_id=peer, device_id_type=MESH)

    block_rows, block_cols = pattern.shape
    low = lax.broadcasted_iota(jnp.int32, (block_cols, width), 0) * BLK
    at = lax.broadcasted_iota(jnp.int32, (block_cols, width), 1)
    spread = jnp.where((at >= low) & (at < low + BLK), 1.0, 0.0).astype(jnp.bfloat16)
    loads[0].wait()
    wide = jnp.dot(
        blocks[...].astype(jnp.float32).astype(jnp.bfloat16), spread,
        preferred_element_type=jnp.float32,
    )
    mask[...] = wide
    for t in range(share * tiles):
        mask_tiles[t] = wide[:, t * LANES:(t + 1) * LANES]
    base = pl.multiple_of(row * rows, rows)
    for t in range(tiles):
        loads[1 + t].wait()
        for i in range(block_rows):
            keep = mask_tiles[half * tiles + t, i:i + 1, :]
            keep = jnp.broadcast_to(keep, (BLK, LANES)).astype(jnp.bfloat16)
            cols[t, pl.ds(base + i * BLK, BLK), :] = raw_cols[t, i * BLK:(i + 1) * BLK, :] * keep

    pl.semaphore_wait(barrier, len(greeted))

    def copy(src, dst, send, recv, to):
        return pltpu.make_async_remote_copy(
            src_ref=src, dst_ref=dst, send_sem=send, recv_sem=recv,
            device_id=to, device_id_type=MESH,
        )

    def arrived(ref, recv):
        copy(ref, ref, own_send, recv, sib).wait_recv()

    def piece(r, t):
        return cols.at[t, pl.ds(pl.multiple_of(r * rows, rows), rows), :]

    sent, flying = [], {}

    def send(*args):
        c = copy(*args)
        c.start()
        sent.append(c)

    def start_y(t):
        for j in range(1, n_y):
            c = copy(piece(row, t), piece(row, t), y_send.at[j - 1, t], y_recv.at[j - 1, t],
                     y_peers[j - 1])
            c.start()
            flying[t, j] = c

    for t in range(min(AHEAD, tiles)):
        start_y(t)
    if cores > 1:
        ref = cols.at[:, pl.ds(base, rows), :]
        send(ref, ref, own_send, own_recv, sib)

    loads[1 + tiles].wait()
    first = depth - half
    for b in range(pair // BLK):
        keep = mask[pl.ds(first * (strip // BLK) + b, 1), :]
        keep = jnp.broadcast_to(keep, (16, width)).astype(jnp.bfloat16)
        for q in range(b * BLK, (b + 1) * BLK, 16):
            left[q:q + 16, pl.ds(pl.multiple_of(col * width, width), width)] = (
                raw_left[q:q + 16, :] * keep)

    step = width // STEPS

    def slab(c, h, k):
        return left.at[pl.ds(pl.multiple_of(h * strip, strip), strip),
                       pl.ds(pl.multiple_of(c * width + k * step, step), step)]

    for k in range(STEPS):
        for j in range(1, n_col):
            send(slab(col, half, k), slab(col, half, k), x_send.at[j - 1, k],
                 x_recv.at[j - 1, k], x_peers[j - 1])

    def take_x(j, k):
        c = lax.rem(col + n_col - j, n_col)
        arrived(slab(c, half, k), x_recv.at[j - 1, k])
        if share > 1:
            send(slab(c, half, k), slab(c, half, k), z_send.at[j - 1, k],
                 z_recv.at[j - 1, k], mate_at)

    def take_z(j, k):
        if share > 1:
            c = lax.rem(col + n_col - j, n_col)
            arrived(slab(c, 1 - half, k), z_recv.at[j - 1, k])

    def take_y(j, t):
        r = lax.rem(y + n_y - j, n_y) * cores + core
        arrived(piece(r, t), y_recv.at[j - 1, t])
        if cores > 1:
            send(piece(r, t), piece(r, t), s_send.at[j - 1, t], s_recv.at[j - 1, t], sib)

    def make(t, which):
        if cores > 1 and which[0] == 0:
            for j in range(1, n_y):
                r = lax.rem(y + n_y - j, n_y) * cores + (cores - 1 - core)
                arrived(piece(r, t), s_recv.at[j - 1, t])
        tile = half * tiles + t
        blocks_here = strip // BLK
        for s in which:
            who = (1 - half) if s == 0 and share > 1 else half
            begin = pl.multiple_of(who * strip, strip)
            product = jnp.dot(left[pl.ds(begin, strip), :], cols[t],
                              preferred_element_type=jnp.float32)
            for b in range(blocks_here):
                keep = mask_tiles[tile, pl.ds((first + who) * blocks_here + b, 1), :]
                value = (product[b * BLK:(b + 1) * BLK, :] * keep).astype(out.dtype)
                if s == 0 and share > 1:
                    given[t, b * BLK:(b + 1) * BLK, :] = value
                else:
                    made[tile, b * BLK:(b + 1) * BLK, :] = value
            if s == 0 and share > 1:
                send(given.at[t], made.at[tile], o_send.at[t], o_recv.at[t], mate_at)

    def forward_x(lo, hi):
        for k in range(lo, min(hi, STEPS)):
            for j in range(1, n_col):
                take_x(j, k)

    def settle():
        for k in range(STEPS):
            for j in range(1, n_col):
                take_z(j, k)
        if cores > 1:
            arrived(cols.at[:, pl.ds(pl.multiple_of(sibling * rows, rows), rows), :], own_recv)

    per = STEPS // 2
    for t in range(tiles):
        if t < 2:
            forward_x(t * per, t * per + per // 2)
        if t == tiles - 1:
            settle()
            for q in range(EARLY):
                make(q, range(share))
        for j in range(1, n_y):
            take_y(j, t)
            flying[t, j].wait_send()
        if t + AHEAD < tiles:
            start_y(t + AHEAD)
        if t < 2:
            forward_x(t * per + per // 2, t * per + per)
    for q in range(EARLY, tiles - 1):
        make(q, (0,))
    make(tiles - 1, (0,))
    if share > 1:
        for q in range(EARLY, tiles):
            make(q, (1,))
    if share > 1:
        for t in range(tiles):
            arrived(made.at[(1 - half) * tiles + t], o_recv.at[t])
    for t in range(share * tiles):
        out[:, t * LANES:(t + 1) * LANES] = made[t]
    for c in sent:
        c.wait_send()


def shards(n_row, n_col, n_depth, density, pattern):
    rows, width = density.shape
    strip = rows // n_depth
    cores, share, n_y = layout(n_row, n_depth)
    tiles = width // share // LANES
    dma = pltpu.SemaphoreType.DMA
    i, j = max(n_col - 1, 1), max(n_y - 1, 1)
    bf16 = jnp.bfloat16
    density = pltpu.with_memory_space_constraint(density, pltpu.HBM)
    pattern = pltpu.with_memory_space_constraint(pattern, pltpu.HBM)
    return pl.pallas_call(
        functools.partial(kernel, n_row, n_col, n_depth),
        out_shape=jax.ShapeDtypeStruct((strip, width), bf16),
        in_specs=[pl.BlockSpec(memory_space=pltpu.HBM)] * 2,
        out_specs=pl.BlockSpec(memory_space=pltpu.VMEM),
        scratch_shapes=[
            pltpu.VMEM((tiles, rows, LANES), bf16),
            pltpu.VMEM((share * strip, width), bf16),
            pltpu.VMEM(pattern.shape, jnp.int32),
            pltpu.VMEM((tiles, n_row * rows, LANES), bf16),
            pltpu.VMEM((share * strip, n_col * width), bf16),
            pltpu.VMEM((pattern.shape[0], width), jnp.float32),
            pltpu.VMEM((share * tiles, pattern.shape[0], LANES), jnp.float32),
            pltpu.VMEM((tiles, strip, LANES), bf16),
            pltpu.VMEM((share * tiles, strip, LANES), bf16),
            dma((tiles + 2,)),
            dma((i, STEPS)), dma((i, STEPS)),
            dma((j, tiles)), dma((j, tiles)),
            dma((i, STEPS)), dma((i, STEPS)),
            dma(()), dma(()),
            dma((j, tiles)), dma((j, tiles)),
            dma((tiles,)), dma((tiles,)),
        ],
        compiler_params=pltpu.CompilerParams(
            collective_id=0, has_side_effects=True, vmem_limit_bytes=32 * 1024 * 1024
        ),
    )(density, pattern)


def solution(mesh):
    sizes = [mesh.shape[name] for name in ("row", "col", "depth")]
    return jax.shard_map(
        functools.partial(shards, *sizes),
        mesh=mesh,
        in_specs=(P("row", "col"), P("row", "col")),
        out_specs=P(("row", "depth"), "col"),
        check_vma=False,
    )
```

```python
import functools

import jax
import jax.numpy as jnp
from jax import lax
from jax.experimental import pallas as pl
from jax.experimental.pallas import tpu as pltpu
from jax.sharding import PartitionSpec as P

BLK = 64
LANES = 128
STEPS = 4
EARLY = 3
AHEAD = 2
MESH = pl.DeviceIdType.MESH


def layout(n_row, n_depth):
    cores = 2 if n_row % 2 == 0 else 1
    share = 2 if n_depth % 2 == 0 else 1
    return cores, share, n_row // cores


def kernel(
    n_row, n_col, n_depth,
    density, pattern, out,
    raw_cols, raw_left, blocks, cols, left, mask, mask_tiles, given, made,
    load_sem, x_send, x_recv, y_send, y_recv, z_send, z_recv, own_send, own_recv,
    s_send, s_recv, o_send, o_recv,
):
    rows, width = density.shape
    strip = rows // n_depth
    cores, share, n_y = layout(n_row, n_depth)
    pair = strip * share
    tiles = width // share // LANES
    row, col, depth = lax.axis_index("row"), lax.axis_index("col"), lax.axis_index("depth")
    y, core = row // cores, row % cores
    half = depth % share
    sibling = y * cores + (cores - 1 - core)
    mate = depth - half + (share - 1 - half)

    y_peers = [(lax.rem(y + j, n_y) * cores + core, col, depth) for j in range(1, n_y)]
    x_peers = [(row, lax.rem(col + j, n_col), depth) for j in range(1, n_col)]
    sib = (sibling, col, depth)
    mate_at = (row, col, mate)
    greeted = y_peers + x_peers + [sib] * (cores > 1) + [mate_at] * (share > 1)

    pair_base = pl.multiple_of((depth - half) * strip, pair)
    loads = [pltpu.make_async_copy(pattern, blocks, load_sem.at[0])]
    for t in range(tiles):
        lane = pl.multiple_of((half * tiles + t) * LANES, LANES)
        loads.append(pltpu.make_async_copy(
            density.at[:, pl.ds(lane, LANES)], raw_cols.at[t], load_sem.at[1 + t]))
    loads.append(pltpu.make_async_copy(
        density.at[pl.ds(pair_base, pair), :], raw_left, load_sem.at[1 + tiles]))
    for c in loads:
        c.start()
    barrier = pltpu.get_barrier_semaphore()
    for peer in greeted:
        pl.semaphore_signal(barrier, inc=1, device_id=peer, device_id_type=MESH)

    block_rows, block_cols = pattern.shape
    low = lax.broadcasted_iota(jnp.int32, (block_cols, width), 0) * BLK
    at = lax.broadcasted_iota(jnp.int32, (block_cols, width), 1)
    spread = jnp.where((at >= low) & (at < low + BLK), 1.0, 0.0).astype(jnp.bfloat16)
    loads[0].wait()
    wide = jnp.dot(
        blocks[...].astype(jnp.float32).astype(jnp.bfloat16), spread,
        preferred_element_type=jnp.float32,
    )
    mask[...] = wide
    for t in range(share * tiles):
        mask_tiles[t] = wide[:, t * LANES:(t + 1) * LANES]
    base = pl.multiple_of(row * rows, rows)
    for t in range(tiles):
        loads[1 + t].wait()
        for i in range(block_rows):
            keep = mask_tiles[half * tiles + t, i:i + 1, :]
            keep = jnp.broadcast_to(keep, (BLK, LANES)).astype(jnp.bfloat16)
            cols[t, pl.ds(base + i * BLK, BLK), :] = raw_cols[t, i * BLK:(i + 1) * BLK, :] * keep

    pl.semaphore_wait(barrier, len(greeted))

    def copy(src, dst, send, recv, to):
        return pltpu.make_async_remote_copy(
            src_ref=src, dst_ref=dst, send_sem=send, recv_sem=recv,
            device_id=to, device_id_type=MESH,
        )

    def arrived(ref, recv):
        copy(ref, ref, own_send, recv, sib).wait_recv()

    def piece(r, t):
        return cols.at[t, pl.ds(pl.multiple_of(r * rows, rows), rows), :]

    sent, flying = [], {}

    def send(*args):
        c = copy(*args)
        c.start()
        sent.append(c)

    def start_y(t):
        for j in range(1, n_y):
            c = copy(piece(row, t), piece(row, t), y_send.at[j - 1, t], y_recv.at[j - 1, t],
                     y_peers[j - 1])
            c.start()
            flying[t, j] = c

    for t in range(min(AHEAD, tiles)):
        start_y(t)
    if cores > 1:
        ref = cols.at[:, pl.ds(base, rows), :]
        send(ref, ref, own_send, own_recv, sib)

    loads[1 + tiles].wait()
    first = depth - half
    for b in range(pair // BLK):
        keep = mask[pl.ds(first * (strip // BLK) + b, 1), :]
        keep = jnp.broadcast_to(keep, (16, width)).astype(jnp.bfloat16)
        for q in range(b * BLK, (b + 1) * BLK, 16):
            left[q:q + 16, pl.ds(pl.multiple_of(col * width, width), width)] = (
                raw_left[q:q + 16, :] * keep)

    step = width // STEPS

    def slab(c, h, k):
        return left.at[pl.ds(pl.multiple_of(h * strip, strip), strip),
                       pl.ds(pl.multiple_of(c * width + k * step, step), step)]

    for k in range(STEPS):
        for j in range(1, n_col):
            send(slab(col, half, k), slab(col, half, k), x_send.at[j - 1, k],
                 x_recv.at[j - 1, k], x_peers[j - 1])

    def take_x(j, k):
        c = lax.rem(col + n_col - j, n_col)
        arrived(slab(c, half, k), x_recv.at[j - 1, k])
        if share > 1:
            send(slab(c, half, k), slab(c, half, k), z_send.at[j - 1, k],
                 z_recv.at[j - 1, k], mate_at)

    def take_z(j, k):
        if share > 1:
            c = lax.rem(col + n_col - j, n_col)
            arrived(slab(c, 1 - half, k), z_recv.at[j - 1, k])

    def take_y(j, t):
        r = lax.rem(y + n_y - j, n_y) * cores + core
        arrived(piece(r, t), y_recv.at[j - 1, t])
        if cores > 1:
            send(piece(r, t), piece(r, t), s_send.at[j - 1, t], s_recv.at[j - 1, t], sib)

    def make(t, which):
        if cores > 1 and which[0] == 0:
            for j in range(1, n_y):
                r = lax.rem(y + n_y - j, n_y) * cores + (cores - 1 - core)
                arrived(piece(r, t), s_recv.at[j - 1, t])
        tile = half * tiles + t
        blocks_here = strip // BLK
        for s in which:
            who = (1 - half) if s == 0 and share > 1 else half
            begin = pl.multiple_of(who * strip, strip)
            product = jnp.dot(left[pl.ds(begin, strip), :], cols[t],
                              preferred_element_type=jnp.float32)
            for b in range(blocks_here):
                keep = mask_tiles[tile, pl.ds((first + who) * blocks_here + b, 1), :]
                value = (product[b * BLK:(b + 1) * BLK, :] * keep).astype(out.dtype)
                if s == 0 and share > 1:
                    given[t, b * BLK:(b + 1) * BLK, :] = value
                else:
                    made[tile, b * BLK:(b + 1) * BLK, :] = value
            if s == 0 and share > 1:
                send(given.at[t], made.at[tile], o_send.at[t], o_recv.at[t], mate_at)

    def forward_x(lo, hi):
        for k in range(lo, min(hi, STEPS)):
            for j in range(1, n_col):
                take_x(j, k)

    def settle():
        for k in range(STEPS):
            for j in range(1, n_col):
                take_z(j, k)
        if cores > 1:
            arrived(cols.at[:, pl.ds(pl.multiple_of(sibling * rows, rows), rows), :], own_recv)

    per = STEPS // 2
    for t in range(tiles):
        if t < 2:
            forward_x(t * per, t * per + per // 2)
        if t == tiles - 1:
            settle()
            for q in range(EARLY):
                make(q, (0,))
        for j in range(1, n_y):
            take_y(j, t)
            flying[t, j].wait_send()
        if t + AHEAD < tiles:
            start_y(t + AHEAD)
        if t < 2:
            forward_x(t * per + per // 2, t * per + per)
    for q in range(EARLY, tiles - 1):
        make(q, (0,))
    make(tiles - 1, (0,))
    if share > 1:
        for q in range(tiles):
            make(q, (1,))
    if share > 1:
        for t in range(tiles):
            arrived(made.at[(1 - half) * tiles + t], o_recv.at[t])
    for t in range(share * tiles):
        out[:, t * LANES:(t + 1) * LANES] = made[t]
    for c in sent:
        c.wait_send()


def shards(n_row, n_col, n_depth, density, pattern):
    rows, width = density.shape
    strip = rows // n_depth
    cores, share, n_y = layout(n_row, n_depth)
    tiles = width // share // LANES
    dma = pltpu.SemaphoreType.DMA
    i, j = max(n_col - 1, 1), max(n_y - 1, 1)
    bf16 = jnp.bfloat16
    density = pltpu.with_memory_space_constraint(density, pltpu.HBM)
    pattern = pltpu.with_memory_space_constraint(pattern, pltpu.HBM)
    return pl.pallas_call(
        functools.partial(kernel, n_row, n_col, n_depth),
        out_shape=jax.ShapeDtypeStruct((strip, width), bf16),
        in_specs=[pl.BlockSpec(memory_space=pltpu.HBM)] * 2,
        out_specs=pl.BlockSpec(memory_space=pltpu.VMEM),
        scratch_shapes=[
            pltpu.VMEM((tiles, rows, LANES), bf16),
            pltpu.VMEM((share * strip, width), bf16),
            pltpu.VMEM(pattern.shape, jnp.int32),
            pltpu.VMEM((tiles, n_row * rows, LANES), bf16),
            pltpu.VMEM((share * strip, n_col * width), bf16),
            pltpu.VMEM((pattern.shape[0], width), jnp.float32),
            pltpu.VMEM((share * tiles, pattern.shape[0], LANES), jnp.float32),
            pltpu.VMEM((tiles, strip, LANES), bf16),
            pltpu.VMEM((share * tiles, strip, LANES), bf16),
            dma((tiles + 2,)),
            dma((i, STEPS)), dma((i, STEPS)),
            dma((j, tiles)), dma((j, tiles)),
            dma((i, STEPS)), dma((i, STEPS)),
            dma(()), dma(()),
            dma((j, tiles)), dma((j, tiles)),
            dma((tiles,)), dma((tiles,)),
        ],
        compiler_params=pltpu.CompilerParams(
            collective_id=0, has_side_effects=True, vmem_limit_bytes=32 * 1024 * 1024
        ),
    )(density, pattern)


def solution(mesh):
    sizes = [mesh.shape[name] for name in ("row", "col", "depth")]
    return jax.shard_map(
        functools.partial(shards, *sizes),
        mesh=mesh,
        in_specs=(P("row", "col"), P("row", "col")),
        out_specs=P(("row", "depth"), "col"),
        check_vma=False,
    )
```
